32 devices in a mesh: fsdp: 8 (over z, y), tp: 4 (over x, core).
Axes of the slice: x: 2, y: 2, z: 4, core: 2. Of those that a mesh axis runs over, the one named last changes fastest.
Arguments:
- tokens: bfloat16 [2048, 4096], P('fsdp', 'tp'), may hold values from -6 to 6
- cotangent: bfloat16 [2048, 4096], P('fsdp', 'tp'), may hold values from -6 to 6
- up_weight: bfloat16 [4096, 14336], P('fsdp', 'tp'), may hold values from -0.1875 to 0.1875
- down_weight: bfloat16 [4096, 14336], P('fsdp', 'tp'), may hold values from -0.09375 to 0.09375
- up_list: int32 [4, 256, 2], P('tp'), may hold values from 0 to 31, as said below
- up_count: int32 [4], P('tp'), may hold values from 60 to 256, as said below
- down_list: int32 [4, 256, 2], P('tp'), may hold values from 0 to 31, as said below
- down_count: int32 [4], P('tp'), may hold values from 60 to 256, as said below
Outputs:
- mixed: bfloat16 [2048, 4096], P('fsdp', 'tp')
- grad_tokens: bfloat16 [2048, 4096], P('fsdp', 'tp')
- grad_up: float32 [4096, 14336], P('fsdp', 'tp')
- grad_down: float32 [4096, 14336], P('fsdp', 'tp')
The draws below stay inside these ranges and needn't reach their ends.
Inputs may be any that keep to these rules, and one draw needn't show every extreme that they name: `up_list`: in each slice's list the first count entries are distinct pairs (row block below 32, column block below 28), in no particular order; every row block has at least one and at most 8 of them; in every slice all 4 row blocks held by some index of fsdp have exactly 8, and in some slice every row block has exactly 8. Entries from the count on are arbitrary pairs in range and carry no meaning. `up_count`: the number of valid entries of each slice's up list. `down_list`: as for up_list. `down_count`: the number of valid entries of each slice's down list.
All inputs are finite; a program needn't handle non-finite values.
Results may differ from the reference program's by a relative error of at most 0.015.
Values may be sent and summed in bfloat16 or wider, within the bound.
A program may use at most 256 MiB of HBM per device.

```python
import jax
import jax.numpy as jnp
from jax import lax

D = 4096
FF = 14336
BLK = 128
GROUP_TOK = 256
TOKENS = 2048
DB = 32
FBT = 28
RB = 4
CAPR = 8
LIST = 256
N_FSDP = 8
N_TP = 4


def list_draw(key, salt):
    folded = jax.random.fold_in(key, salt)
    keys = jax.random.split(folded, 7)
    counts = jax.random.randint(keys[0], (N_TP, DB), 1, CAPR + 1)
    full_owner = jax.random.randint(keys[1], (N_TP, 1), 0, N_FSDP)
    row_ids = jnp.arange(DB, dtype=jnp.int32)[None, :]
    counts = jnp.where(row_ids // RB == full_owner, CAPR, counts)
    full_slice = jax.random.randint(keys[6], (), 0, N_TP)
    slice_ids = jnp.arange(N_TP, dtype=jnp.int32)[:, None]
    counts = jnp.where(slice_ids == full_slice, CAPR, counts)
    perm_keys = jax.random.split(keys[2], N_TP * DB)
    perms = jax.vmap(lambda single: jax.random.permutation(single, FBT))(perm_keys)
    chosen = perms.reshape(N_TP, DB, FBT)[:, :, :CAPR].astype(jnp.int32)
    valid = jnp.arange(CAPR, dtype=jnp.int32)[None, None, :] < counts[:, :, None]
    rows = jnp.broadcast_to(jnp.arange(DB, dtype=jnp.int32)[None, :, None], (N_TP, DB, CAPR))
    rows = rows.reshape(N_TP, LIST)
    cols = chosen.reshape(N_TP, LIST)
    valid = valid.reshape(N_TP, LIST)
    scores = jax.random.randint(keys[3], (N_TP, LIST), 0, 1 << 20)
    scores = jnp.where(valid, scores, 1 << 20) * LIST + jnp.arange(LIST, dtype=jnp.int32)[None, :]
    order = jnp.argsort(scores, axis=1)
    rows = jnp.take_along_axis(rows, order, axis=1)
    cols = jnp.take_along_axis(cols, order, axis=1)
    valid = jnp.take_along_axis(valid, order, axis=1)
    filler_rows = jax.random.randint(keys[4], (N_TP, LIST), 0, DB)
    filler_cols = jax.random.randint(keys[5], (N_TP, LIST), 0, FBT)
    rows = jnp.where(valid, rows, filler_rows)
    cols = jnp.where(valid, cols, filler_cols)
    entries = jnp.stack([rows, cols], axis=-1).astype(jnp.int32)
    number = jnp.sum(valid.astype(jnp.int32), axis=1).astype(jnp.int32)
    return (entries, number)


def draw_up_list(key, part):
    return list_draw(key, 11)[0]


def draw_up_count(key, part):
    return list_draw(key, 11)[1]


def draw_down_list(key, part):
    return list_draw(key, 23)[0]


def draw_down_count(key, part):
    return list_draw(key, 23)[1]


def with_spikes(values, own_key, source, target, blocks, factor):
    owner, partner = [(jnp.arange(values.shape[position]) // (values.shape[position] // blocks)).reshape([-1 if axis == position else 1 for axis in range(values.ndim)]) for position in (source, target)]
    chosen = jax.random.permutation(own_key, blocks)[partner]
    strong = (owner == chosen) | (owner == (partner + blocks // 2) % blocks)
    return jnp.where(strong, factor * values, values)


def steps_of(stream_key, extent, shards, smallest, top_value):
    factor_of = 1.0
    for axis_at, blocks in shards:
        heights = jax.random.uniform(jax.random.fold_in(jax.random.fold_in(stream_key, 6), axis_at), (blocks,), jnp.float32, smallest / len(shards), top_value / len(shards))
        factor_of = factor_of * jnp.repeat(jnp.exp(heights), extent[axis_at] // blocks).reshape((-1,) + (1,) * (len(extent) - 1 - axis_at))
    return factor_of


def gaussian(own_key, dims, scale, limit, cuts=(), kind=jnp.bfloat16):
    values = scale * jax.random.normal(own_key, dims, jnp.float32)
    if cuts:
        values = values * steps_of(own_key, dims, cuts, -0.22, 0.18)
    return jnp.clip(values, -limit, limit).astype(kind)


def gaussian_with(stream_key, dims, scale, most, pieces, heavy, held_as=jnp.bfloat16):
    array = scale * jax.random.normal(stream_key, dims, jnp.float32)
    if pieces:
        array = array * steps_of(stream_key, dims, pieces, -0.22, 0.18)
    return jnp.clip(with_spikes(array, jax.random.fold_in(stream_key, 3), *heavy), -most, most).astype(held_as)


def setup_inputs(seed: int = 0) -> dict:
    key_of = jax.random.split(jax.random.key(seed), 9)
    tokens = gaussian_with(key_of[0], (TOKENS, D), 1.0, 6.0, ((0, 8), (1, 4)), (0, 1, 8, 2.0))
    cotangent = gaussian_with(key_of[1], (TOKENS, D), 1.0, 6.0, ((0, 8), (1, 4)), (0, 1, 8, 2.0))
    up_weight = gaussian(key_of[2], (D, FF), (D // 4) ** -0.5, 0.1875, ((0, 8), (1, 4)))
    down_weight = gaussian(key_of[3], (D, FF), (FF // 4) ** -0.5, 0.09375, ((0, 8), (1, 4)))
    up_list = draw_up_list(jax.random.fold_in(key_of[8], 71), 0)
    up_count = draw_up_count(jax.random.fold_in(key_of[8], 71), 0)
    down_list = draw_down_list(jax.random.fold_in(key_of[8], 71), 0)
    down_count = draw_down_count(jax.random.fold_in(key_of[8], 71), 0)
    return {"tokens": tokens, "cotangent": cotangent, "up_weight": up_weight, "down_weight": down_weight, "up_list": up_list, "up_count": up_count, "down_list": down_list, "down_count": down_count}


SQRT_TWO_PI = 0.7978845608028654
CUBIC = 0.044715


def gelu_tanh(values):
    inner = SQRT_TWO_PI * (values + CUBIC * values * values * values)
    return 0.5 * values * (1.0 + jnp.tanh(inner))


def gelu_slope(values):
    tangent = jnp.tanh(SQRT_TWO_PI * (values + CUBIC * values * values * values))
    return 0.5 * (1.0 + tangent) + 0.5 * values * (1.0 - tangent * tangent) * SQRT_TWO_PI * (1.0 + 3.0 * CUBIC * values * values)


def list_tables(entries, number):
    rows = entries[:, :, 0].astype(jnp.int32)
    offsets = (jnp.arange(N_TP, dtype=jnp.int32) * FBT)[:, None]
    cols = entries[:, :, 1].astype(jnp.int32) + offsets
    valid = jnp.arange(LIST, dtype=jnp.int32)[None, :] < number[:, None]
    return rows, cols, valid


def blocks_of(weight, rows, cols, valid):
    tiles = weight.reshape(DB, BLK, FF // BLK, BLK)
    picked = tiles[rows, :, cols, :]
    return jnp.where(valid[:, :, None, None], picked, jnp.zeros((), weight.dtype))


def rounded_sum(parts):
    narrow = lax.optimization_barrier(parts.astype(jnp.bfloat16))
    return jnp.sum(narrow.astype(jnp.float32), axis=1)


def reference(tokens, cotangent, up_weight, down_weight, up_list, up_count, down_list, down_count):
    up_rows, up_cols, up_valid = list_tables(up_list, up_count)
    down_rows, down_cols, down_valid = list_tables(down_list, down_count)
    up_tiles = blocks_of(up_weight, up_rows, up_cols, up_valid).astype(jnp.float32)
    down_tiles = blocks_of(down_weight, down_rows, down_cols, down_valid).astype(jnp.float32)
    slice_ids = jnp.arange(N_TP, dtype=jnp.int32)[:, None]
    token_groups = tokens.reshape(N_FSDP, GROUP_TOK, D)
    grad_groups = cotangent.reshape(N_FSDP, GROUP_TOK, D)

    def group_step(carry, group):
        x_group, dy_group = group
        x_tiles = x_group.reshape(GROUP_TOK, DB, BLK)
        dy_tiles = dy_group.reshape(GROUP_TOK, DB, BLK)
        x_taken = x_tiles[:, up_rows, :].astype(jnp.float32)
        partial_up = jnp.einsum('rtlk,tlkn->rtln', x_taken, up_tiles)
        hidden = jnp.zeros((GROUP_TOK, FF // BLK, BLK), jnp.float32).at[:, up_cols, :].add(partial_up)
        active = gelu_tanh(hidden).astype(jnp.bfloat16)
        active_taken = active[:, down_cols, :].astype(jnp.float32)
        partial_down = jnp.einsum('rtln,tlkn->rtlk', active_taken, down_tiles)
        layer_parts = jnp.zeros((GROUP_TOK, N_TP, DB, BLK), jnp.float32).at[:, slice_ids, down_rows, :].add(partial_down)
        mixed = rounded_sum(layer_parts).reshape(GROUP_TOK, D).astype(jnp.bfloat16)
        dy_taken = dy_tiles[:, down_rows, :].astype(jnp.float32)
        back_down = jnp.einsum('rtlk,tlkn->rtln', dy_taken, down_tiles)
        grad_active = jnp.zeros((GROUP_TOK, FF // BLK, BLK), jnp.float32).at[:, down_cols, :].add(back_down)
        grad_hidden = (grad_active * gelu_slope(hidden)).astype(jnp.bfloat16)
        hidden_taken = grad_hidden[:, up_cols, :].astype(jnp.float32)
        back_up = jnp.einsum('rtln,tlkn->rtlk', hidden_taken, up_tiles)
        input_parts = jnp.zeros((GROUP_TOK, N_TP, DB, BLK), jnp.float32).at[:, slice_ids, up_rows, :].add(back_up)
        grad_tokens = rounded_sum(input_parts).reshape(GROUP_TOK, D).astype(jnp.bfloat16)
        up_term = jnp.einsum('rtlk,rtln->tlkn', x_taken, hidden_taken)
        down_term = jnp.einsum('rtlk,rtln->tlkn', dy_taken, active_taken)
        up_term = lax.optimization_barrier(up_term.astype(jnp.bfloat16)).astype(jnp.float32)
        down_term = lax.optimization_barrier(down_term.astype(jnp.bfloat16)).astype(jnp.float32)
        return (carry[0] + up_term, carry[1] + down_term), (mixed, grad_tokens)

    start_sums = (jnp.zeros((N_TP, LIST, BLK, BLK), jnp.float32), jnp.zeros((N_TP, LIST, BLK, BLK), jnp.float32))
    sums, outputs = lax.scan(group_step, start_sums, (token_groups, grad_groups))
    mixed = outputs[0].reshape(TOKENS, D)
    grad_tokens = outputs[1].reshape(TOKENS, D)
    up_sum = jnp.where(up_valid[:, :, None, None], sums[0], jnp.zeros((), jnp.float32))
    down_sum = jnp.where(down_valid[:, :, None, None], sums[1], jnp.zeros((), jnp.float32))
    grad_up = jnp.zeros((DB, BLK, FF // BLK, BLK), jnp.float32).at[up_rows, :, up_cols, :].add(up_sum).reshape(D, FF)
    grad_down = jnp.zeros((DB, BLK, FF // BLK, BLK), jnp.float32).at[down_rows, :, down_cols, :].add(down_sum).reshape(D, FF)
    return (mixed, grad_tokens, grad_up, grad_down)
```

```python
import functools

import jax
import jax.numpy as jnp
from jax import lax
from jax.experimental import pallas as pl
from jax.experimental.pallas import tpu as pltpu
from jax.sharding import PartitionSpec as P

BLK = 128
SQRT_TWO_PI = 0.7978845608028654
CUBIC = 0.044715
F32 = jnp.float32
BF16 = jnp.bfloat16


def tables(entries, counts, row_blocks, col_blocks, cap):
    length = entries.shape[1]
    rows, cols = entries[:, :, 0], entries[:, :, 1]
    at = jnp.arange(length, dtype=jnp.int32)
    valid = at[None, :] < counts[:, None]
    earlier = (rows[:, :, None] == rows[:, None, :]) & (at[None, None, :] < at[None, :, None])
    rank = jnp.sum((earlier & valid[:, None, :]).astype(jnp.int32), axis=2)
    slot = jnp.where(valid, rows * cap + rank, -1)
    slots = jnp.arange(row_blocks * cap, dtype=jnp.int32)
    chosen = slot[:, None, :] == slots[None, :, None]
    slot_cols = jnp.sum(jnp.where(chosen, cols[:, None, :] + 1, 0), axis=2) - 1
    place = jnp.where(valid, rows * col_blocks + cols, -1)
    places = jnp.arange(row_blocks * col_blocks, dtype=jnp.int32)
    here = place[:, None, :] == places[None, :, None]
    rank_of = jnp.sum(jnp.where(here, rank[:, None, :] - cap, 0), axis=2) + cap
    return slot_cols, rank_of.reshape(entries.shape[0], row_blocks, col_blocks)


def pick_kernel(cap, cols_ref, up_ref, down_ref, out_ref, sems):
    count = out_ref.shape[0] // 2
    for side, weight in enumerate((up_ref, down_ref)):
        for s in range(count):
            col = pl.multiple_of(jnp.maximum(cols_ref[side, s], 0) * BLK, BLK)
            pltpu.make_async_copy(
                weight.at[pl.ds((s // cap) * BLK, BLK), pl.ds(col, BLK)],
                out_ref.at[side * count + s],
                sems.at[side * count + s],
            ).start()
    for side, weight in enumerate((up_ref, down_ref)):
        for s in range(count):
            pltpu.make_async_copy(
                weight.at[pl.ds((s // cap) * BLK, BLK), pl.ds(0, BLK)],
                out_ref.at[side * count + s],
                sems.at[side * count + s],
            ).wait()

            @pl.when(cols_ref[side, s] < 0)
            def _():
                out_ref[side * count + s] = jnp.zeros((BLK, BLK), BF16)


def pick(cols, up_weight, down_weight, cap):
    count = cols.shape[1]
    return pl.pallas_call(
        functools.partial(pick_kernel, cap),
        out_shape=jax.ShapeDtypeStruct((2 * count, BLK, BLK), BF16),
        in_specs=[
            pl.BlockSpec(memory_space=pltpu.SMEM),
            pl.BlockSpec(memory_space=pl.ANY),
            pl.BlockSpec(memory_space=pl.ANY),
        ],
        out_specs=pl.BlockSpec(memory_space=pltpu.VMEM),
        scratch_shapes=[pltpu.SemaphoreType.DMA((2 * count,))],
        name="pick_blocks",
    )(cols, up_weight, down_weight)


def place_kernel(cap, cols_ref, sum_ref, up_ref, down_ref):
    row = pl.program_id(0)
    for side, out in enumerate((up_ref, down_ref)):
        out[...] = jnp.zeros_like(out)
        for j in range(cap):
            col = cols_ref[side, row * cap + j]

            @pl.when(col >= 0)
            def _():
                out[:, pl.ds(pl.multiple_of(col * BLK, BLK), BLK)] = sum_ref[side, j].astype(F32)


def place(cols, summed, cap, col_blocks):
    count = cols.shape[1]
    spec = pl.BlockSpec((BLK, col_blocks * BLK), lambda r: (r, 0))
    shape = jax.ShapeDtypeStruct((count // cap * BLK, col_blocks * BLK), F32)
    return pl.pallas_call(
        functools.partial(place_kernel, cap),
        grid=(count // cap,),
        out_shape=(shape, shape),
        in_specs=[
            pl.BlockSpec(memory_space=pltpu.SMEM),
            pl.BlockSpec((2, cap, BLK, BLK), lambda r: (0, r, 0, 0)),
        ],
        out_specs=(spec, spec),
        compiler_params=pltpu.CompilerParams(vmem_limit_bytes=32 << 20),
        name="place_grads",
    )(cols, summed)


MESH = pl.DeviceIdType.MESH
PIECES = 4


def dot_t(left, right):
    return lax.dot_general(left, right, (((1,), (1,)), ((), ())), preferred_element_type=F32)


def fused_kernel(
    n, ways, per, cap, cols, rank, picked, tokens, cotangent,
    mixed, grad_tokens, summed,
    x, dy, wu, wd, stage, hid, grad, act, gh, lay, inp, lay_in, inp_in, first, passing,
    local_sems, tp_send, tp_recv, ag_send, ag_recv, rs_send, rs_recv, back_send, back_recv,
):
    me_f = lax.axis_index("fsdp")
    me_t = lax.axis_index("tp")
    mine = per * cap
    npc = mine // PIECES
    half = max(1, per // 2)
    rowwise = per % PIECES == 0
    pairs = hid.shape[0]
    rows = n * per
    rpt = rows // ways
    width = rpt * BLK

    def at_position(q):
        q = lax.rem(q + 2 * n, n)
        high = q // (n // 2)
        return 2 * q * (1 - high) + (2 * n - 1 - 2 * q) * high

    odd = lax.rem(me_f, 2)
    here = (me_f // 2) * (1 - odd) + (n - 1 - me_f // 2) * odd
    target = (at_position(here + 1), at_position(here - 1))

    barrier = pltpu.get_barrier_semaphore()
    for f in target:
        pl.semaphore_signal(barrier, inc=1, device_id=(f, me_t), device_id_type=MESH)
    for i in range(1, ways):
        pl.semaphore_signal(
            barrier, inc=1, device_id=(me_f, lax.rem(me_t + i, ways)), device_id_type=MESH
        )

    weights = (wu, wd)
    spot = pl.ds(me_f * mine, mine)
    locals_ = [
        pltpu.make_async_copy(picked.at[pl.ds(0, mine)], wu.at[spot], local_sems.at[0]),
        pltpu.make_async_copy(picked.at[pl.ds(mine, mine)], wd.at[spot], local_sems.at[1]),
        pltpu.make_async_copy(tokens, x.at[me_t], local_sems.at[2]),
        pltpu.make_async_copy(cotangent, dy.at[me_t], local_sems.at[3]),
    ]
    for copy in locals_:
        copy.start()
    for copy in locals_:
        copy.wait()
    pl.semaphore_wait(barrier, 2 + ways - 1)

    def features(side, i):
        full = (x, dy)[side]
        return pltpu.make_async_remote_copy(
            src_ref=full.at[me_t],
            dst_ref=full.at[me_t],
            send_sem=tp_send.at[side, i],
            recv_sem=tp_recv.at[side, i],
            device_id=(me_f, lax.rem(me_t + i, ways)),
            device_id_type=MESH,
        )

    def hop(side, step, k, d):
        owner = at_position(here - step if d == 0 else here + step)
        block = weights[side].at[pl.ds(owner * mine + k * npc, npc)]
        return pltpu.make_async_remote_copy(
            src_ref=block,
            dst_ref=block,
            send_sem=ag_send.at[side, step, k],
            recv_sem=ag_recv.at[side, step, k],
            device_id=(target[d], me_t),
            device_id_type=MESH,
        )

    def arrived(side, step, k, d):
        owner = at_position(here - step - 1 if d == 0 else here + step + 1)
        block = weights[side].at[pl.ds(owner * mine + k * npc, npc)]
        return pltpu.make_async_remote_copy(
            src_ref=block,
            dst_ref=block,
            send_sem=ag_send.at[side, step, k],
            recv_sem=ag_recv.at[side, step, k],
            device_id=(target[d], me_t),
            device_id_type=MESH,
        )

    order = [(d * (PIECES // 2) + j, d) for j in range(PIECES // 2) for d in range(2)]

    def gather_start(side):
        for k, d in order:
            hop(side, 0, k, d).start()

    def gather_step(side, step, forward):
        for k, d in order:
            arrived(side, step, k, d).wait_recv()
            if forward:
                hop(side, step + 1, k, d).start()

    def spread(side, row, count):
        total = (hid, grad)[side]
        for i in range(count):
            stage[i, pl.ds(0, cap)] = weights[side][pl.ds((row + i) * cap, cap)]
        full = (x, dy)[side]
        part = full[row // rpt, :, pl.ds(pl.multiple_of(lax.rem(row, rpt) * BLK, BLK), count * BLK)]

        def column(c, carry):
            block = jnp.concatenate(
                [
                    jnp.concatenate(
                        [stage[i, rank[side, row + i, 2 * c + q]] for q in range(2)], axis=1
                    )
                    for i in range(count)
                ],
                axis=0,
            )
            total[c] += jnp.dot(part, block, preferred_element_type=F32)
            return carry

        lax.fori_loop(0, pairs, column, 0)

    def spread_arrived(side, step):
        if rowwise:
            for d in range(2):
                owner = at_position(here - step - 1 if d == 0 else here + step + 1)
                spread(side, owner * per + d * half, half)

    def spread_own(side):
        if rowwise:
            for d in range(2):
                spread(side, me_f * per + d * half, half)

    def spread_all(side):
        if not rowwise:

            def one(r, carry):
                spread(side, r, 1)
                return carry

            lax.fori_loop(0, rows, one, 0)

    def activate(c):
        v = hid[c]
        s = jnp.tanh(SQRT_TWO_PI * (v + CUBIC * v * v * v))
        a = (0.5 * v * (1.0 + s)).astype(BF16)
        act[2 * c] = a[:, :BLK]
        act[2 * c + 1] = a[:, BLK:]
        hid[c] = 0.5 * (1.0 + s) + 0.5 * v * (1.0 - s * s) * SQRT_TWO_PI * (1.0 + 3.0 * CUBIC * v * v)

    def finish(c, carry):
        g = (grad[c] * hid[c]).astype(BF16)
        gh[2 * c] = g[:, :BLK]
        gh[2 * c + 1] = g[:, BLK:]
        return carry

    def taken(side, start, count):
        values = (gh, act)[side]
        return jnp.concatenate([values[cols[side, start + j]] for j in range(count)], axis=1)

    def back(r):
        at = pl.ds(pl.multiple_of(lax.rem(r, rpt) * BLK, BLK), BLK)
        for side, out in ((0, inp), (1, lay)):
            block = jnp.concatenate([weights[side][r * cap + j] for j in range(cap)], axis=1)
            out[r // rpt, :, at] = dot_t(taken(side, r * cap, cap), block).astype(BF16)

    def term(side, owner, k):
        row = owner * per + (k * npc) // cap
        at = pl.ds(pl.multiple_of(lax.rem(row, rpt) * BLK, BLK), BLK)
        left = (x, dy)[side][row // rpt, :, at].T
        return jnp.dot(left, taken(side, owner * mine + k * npc, npc), preferred_element_type=F32)

    def send_sum(side, step, k, d, source):
        return pltpu.make_async_remote_copy(
            src_ref=source,
            dst_ref=passing.at[side, step, k],
            send_sem=rs_send.at[side, step, k],
            recv_sem=rs_recv.at[side, step, k],
            device_id=(target[d], me_t),
            device_id_type=MESH,
        )

    def scatter_start(side):
        for k, d in order:
            value = term(side, at_position(here - 1 if d == 0 else here + 1), k).astype(BF16)
            for j in range(npc):
                first[side, k, j] = value[:, j * BLK : (j + 1) * BLK]
            send_sum(side, 0, k, d, first.at[side, k]).start()

    def scatter_step(side, step):
        for k, d in order:
            value = term(side, at_position(here - step - 2 if d == 0 else here + step + 2), k)
            send_sum(side, step, k, d, passing.at[side, step, k]).wait_recv()
            for j in range(npc):
                passing[side, step, k, j] = (
                    passing[side, step, k, j].astype(F32) + value[:, j * BLK : (j + 1) * BLK]
                ).astype(BF16)
            send_sum(side, step + 1, k, d, passing.at[side, step, k]).start()

    def scatter_last(side):
        for k, d in order:
            value = term(side, me_f, k)
            send_sum(side, n - 2, k, d, passing.at[side, n - 2, k]).wait_recv()
            for j in range(npc):
                summed[side, k * npc + j] = (
                    passing[side, n - 2, k, j].astype(F32) + value[:, j * BLK : (j + 1) * BLK]
                )

    def share(side, i):
        out, into = ((inp, inp_in), (lay, lay_in))[side]
        to = lax.rem(me_t + i, ways)
        return pltpu.make_async_remote_copy(
            src_ref=out.at[to],
            dst_ref=into.at[i - 1],
            send_sem=back_send.at[side, i],
            recv_sem=back_recv.at[side, i],
            device_id=(me_f, to),
            device_id_type=MESH,
        )

    for i in range(1, ways):
        features(0, i).start()
    gather_start(0)
    hid[...] = jnp.zeros_like(hid)
    grad[...] = jnp.zeros_like(grad)
    for i in range(stage.shape[0]):
        stage[i, cap] = jnp.zeros((BLK, BLK), BF16)
    gather_step(0, 0, True)
    gather_step(0, 1, True)
    for i in range(1, ways):
        features(1, i).start()
    for i in range(1, ways):
        features(0, i).wait_recv()
    spread_own(0)

    def up_step(s, carry):
        gather_step(0, s, True)
        spread_arrived(0, s - 2)
        return carry

    lax.fori_loop(2, n - 2, up_step, 0)
    gather_start(1)
    spread_arrived(0, n - 4)
    gather_step(0, n - 2, False)
    spread_arrived(0, n - 3)
    spread_arrived(0, n - 2)
    spread_all(0)
    for i in range(1, ways):
        features(1, i).wait_recv()

    share_act = -(-pairs // (n - 2))

    def down_step(s, carry):
        gather_step(1, s, True)
        for i in range(share_act):

            @pl.when(s * share_act + i < pairs)
            def _():
                activate(s * share_act + i)

        spread_arrived(1, s)
        return carry

    lax.fori_loop(0, n - 2, down_step, 0)
    scatter_start(1)
    spread_own(1)
    gather_step(1, n - 2, False)
    spread_arrived(1, n - 2)
    spread_all(1)
    lax.fori_loop(0, pairs, finish, 0)

    share_rows = -(-rows // (n - 2))

    def down_sum(s, carry):
        scatter_step(1, s)

        def one(r, inner):
            back(r)
            return inner

        lax.fori_loop(s * share_rows, jnp.minimum((s + 1) * share_rows, rows), one, 0)
        return carry

    lax.fori_loop(0, n - 2, down_sum, 0)
    scatter_start(0)
    for side in range(2):
        for i in range(1, ways):
            share(side, i).start()
    scatter_last(1)

    def up_sum(s, carry):
        scatter_step(0, s)
        return carry

    lax.fori_loop(0, n - 2, up_sum, 0)
    for side, out, own, into in ((0, grad_tokens, inp, inp_in), (1, mixed, lay, lay_in)):
        for i in range(1, ways):
            share(side, i).wait_recv()
        total = own[me_t].astype(F32)
        for i in range(1, ways):
            total += into[i - 1].astype(F32)
        out[...] = total.astype(BF16)
    scatter_last(0)

    for side in range(2):
        for i in range(1, ways):
            features(side, i).wait_send()
            share(side, i).wait_send()

        def sent(s, carry):
            for k, d in order:
                hop(side, s, k, d).wait_send()
                send_sum(side, s, k, d, passing.at[side, s, k]).wait_send()
            return carry

        lax.fori_loop(0, n - 1, sent, 0)


def fused(cols, rank, picked, tokens, cotangent, n, ways, per, cap, col_blocks):
    group, width = tokens.shape
    rows = n * per
    npc = per * cap // PIECES
    half = max(1, per // 2)
    vmem = pl.BlockSpec(memory_space=pltpu.VMEM)
    smem = pl.BlockSpec(memory_space=pltpu.SMEM)
    hbm = pl.BlockSpec(memory_space=pl.ANY)
    dma = pltpu.SemaphoreType.DMA
    return pl.pallas_call(
        functools.partial(fused_kernel, n, ways, per, cap),
        out_shape=(
            jax.ShapeDtypeStruct((group, width), BF16),
            jax.ShapeDtypeStruct((group, width), BF16),
            jax.ShapeDtypeStruct((2, per * cap, BLK, BLK), F32),
        ),
        in_specs=[smem, smem, hbm, hbm, hbm],
        out_specs=(vmem, vmem, vmem),
        scratch_shapes=[
            pltpu.VMEM((ways, group, width), BF16),
            pltpu.VMEM((ways, group, width), BF16),
            pltpu.VMEM((rows * cap, BLK, BLK), BF16),
            pltpu.VMEM((rows * cap, BLK, BLK), BF16),
            pltpu.VMEM((half, cap + 1, BLK, BLK), BF16),
            pltpu.VMEM((col_blocks // 2, group, 2 * BLK), F32),
            pltpu.VMEM((col_blocks // 2, group, 2 * BLK), F32),
            pltpu.VMEM((col_blocks, group, BLK), BF16),
            pltpu.VMEM((col_blocks, group, BLK), BF16),
            pltpu.VMEM((ways, group, width), BF16),
            pltpu.VMEM((ways, group, width), BF16),
            pltpu.VMEM((ways - 1, group, width), BF16),
            pltpu.VMEM((ways - 1, group, width), BF16),
            pltpu.VMEM((2, PIECES, npc, BLK, BLK), BF16),
            pltpu.VMEM((2, n - 1, PIECES, npc, BLK, BLK), BF16),
            dma((4,)),
            dma((2, ways)),
            dma((2, ways)),
            dma((2, n - 1, PIECES)),
            dma((2, n - 1, PIECES)),
            dma((2, n - 1, PIECES)),
            dma((2, n - 1, PIECES)),
            dma((2, ways)),
            dma((2, ways)),
        ],
        compiler_params=pltpu.CompilerParams(
            collective_id=0, has_side_effects=True, vmem_limit_bytes=63 << 20
        ),
        name="fused_layer",
    )(cols, rank, picked, tokens, cotangent)


def body(tokens, cotangent, up_weight, down_weight, up_list, up_count, down_list, down_count):
    per = up_weight.shape[0] // BLK
    col_blocks = up_weight.shape[1] // BLK
    owners = lax.axis_size("fsdp")
    rows = per * owners
    cap = up_list.shape[1] // rows
    mine = per * cap
    entries = jnp.stack([up_list[0], down_list[0]])
    counts = jnp.stack([up_count[0], down_count[0]])
    cols, rank = tables(entries, counts, rows, col_blocks, cap)
    my_cols = lax.dynamic_slice_in_dim(cols, lax.axis_index("fsdp") * mine, mine, axis=1)
    picked = pick(my_cols, up_weight, down_weight, cap)
    mixed, grad_tokens, summed = fused(
        jnp.maximum(cols, 0), rank, picked, tokens, cotangent,
        owners, lax.axis_size("tp"), per, cap, col_blocks,
    )
    grad_up, grad_down = place(my_cols, summed, cap, col_blocks)
    return (mixed, grad_tokens, grad_up, grad_down)


def solution(mesh):
    return jax.shard_map(
        body,
        mesh=mesh,
        in_specs=(
            P("fsdp", "tp"),
            P("fsdp", "tp"),
            P("fsdp", "tp"),
            P("fsdp", "tp"),
            P("tp", None, None),
            P("tp"),
            P("tp", None, None),
            P("tp"),
        ),
        out_specs=(P("fsdp", "tp"), P("fsdp", "tp"), P("fsdp", "tp"), P("fsdp", "tp")),
        check_vma=False,
    )
```

```python
import functools

import jax
import jax.numpy as jnp
from jax import lax
from jax.experimental import pallas as pl
from jax.experimental.pallas import tpu as pltpu
from jax.sharding import PartitionSpec as P

BLK = 128
SQRT_TWO_PI = 0.7978845608028654
CUBIC = 0.044715
F32 = jnp.float32
BF16 = jnp.bfloat16


def tables(entries, counts, row_blocks, col_blocks, cap):
    length = entries.shape[1]
    rows, cols = entries[:, :, 0], entries[:, :, 1]
    at = jnp.arange(length, dtype=jnp.int32)
    valid = at[None, :] < counts[:, None]
    earlier = (rows[:, :, None] == rows[:, None, :]) & (at[None, None, :] < at[None, :, None])
    rank = jnp.sum((earlier & valid[:, None, :]).astype(jnp.int32), axis=2)
    slot = jnp.where(valid, rows * cap + rank, -1)
    slots = jnp.arange(row_blocks * cap, dtype=jnp.int32)
    chosen = slot[:, None, :] == slots[None, :, None]
    slot_cols = jnp.sum(jnp.where(chosen, cols[:, None, :] + 1, 0), axis=2) - 1
    place = jnp.where(valid, rows * col_blocks + cols, -1)
    places = jnp.arange(row_blocks * col_blocks, dtype=jnp.int32)
    here = place[:, None, :] == places[None, :, None]
    rank_of = jnp.sum(jnp.where(here, rank[:, None, :] - cap, 0), axis=2) + cap
    return slot_cols, rank_of.reshape(entries.shape[0], row_blocks, col_blocks)


def pick_kernel(cap, cols_ref, up_ref, down_ref, out_ref, sems):
    count = out_ref.shape[0] // 2
    for side, weight in enumerate((up_ref, down_ref)):
        for s in range(count):
            col = pl.multiple_of(jnp.maximum(cols_ref[side, s], 0) * BLK, BLK)
            pltpu.make_async_copy(
                weight.at[pl.ds((s // cap) * BLK, BLK), pl.ds(col, BLK)],
                out_ref.at[side * count + s],
                sems.at[side * count + s],
            ).start()
    for side, weight in enumerate((up_ref, down_ref)):
        for s in range(count):
            pltpu.make_async_copy(
                weight.at[pl.ds((s // cap) * BLK, BLK), pl.ds(0, BLK)],
                out_ref.at[side * count + s],
                sems.at[side * count + s],
            ).wait()

            @pl.when(cols_ref[side, s] < 0)
            def _():
                out_ref[side * count + s] = jnp.zeros((BLK, BLK), BF16)


def pick(cols, up_weight, down_weight, cap):
    count = cols.shape[1]
    return pl.pallas_call(
        functools.partial(pick_kernel, cap),
        out_shape=jax.ShapeDtypeStruct((2 * count, BLK, BLK), BF16),
        in_specs=[
            pl.BlockSpec(memory_space=pltpu.SMEM),
            pl.BlockSpec(memory_space=pl.ANY),
            pl.BlockSpec(memory_space=pl.ANY),
        ],
        out_specs=pl.BlockSpec(memory_space=pltpu.VMEM),
        scratch_shapes=[pltpu.SemaphoreType.DMA((2 * count,))],
        name="pick_blocks",
    )(cols, up_weight, down_weight)


def place_kernel(cap, cols_ref, sum_ref, mixed_in, grad_in, up_ref, down_ref, mixed_out, grad_out):
    row = pl.program_id(0)
    mixed_out[...] = mixed_in[...]
    grad_out[...] = grad_in[...]
    for side, out in enumerate((up_ref, down_ref)):
        out[...] = jnp.zeros_like(out)
        for j in range(cap):
            col = cols_ref[side, row * cap + j]

            @pl.when(col >= 0)
            def _():
                out[:, pl.ds(pl.multiple_of(col * BLK, BLK), BLK)] = sum_ref[side, j]


def place(cols, summed, mixed, grad_tokens, cap, col_blocks):
    count = cols.shape[1]
    per, cuts = count // cap, 2
    group, width = mixed.shape
    depth = BLK // cuts
    spec = pl.BlockSpec((depth, col_blocks * BLK), lambda r, h: (r * cuts + h, 0))
    shape = jax.ShapeDtypeStruct((per * BLK, col_blocks * BLK), F32)
    through = pl.BlockSpec((group // (per * cuts), width), lambda r, h: (r * cuts + h, 0))
    same = jax.ShapeDtypeStruct(mixed.shape, BF16)
    return pl.pallas_call(
        functools.partial(place_kernel, cap),
        grid=(per, cuts),
        out_shape=(shape, shape, same, same),
        in_specs=[
            pl.BlockSpec(memory_space=pltpu.SMEM),
            pl.BlockSpec((2, cap, depth, BLK), lambda r, h: (0, r, h, 0)),
            through,
            through,
        ],
        out_specs=(spec, spec, through, through),
        compiler_params=pltpu.CompilerParams(vmem_limit_bytes=60 << 20),
        name="place_grads",
    )(cols, summed, mixed, grad_tokens)


MESH = pl.DeviceIdType.MESH
PIECES = 4


def dot_t(left, right):
    return lax.dot_general(left, right, (((1,), (1,)), ((), ())), preferred_element_type=F32)


def fused_kernel(
    n, ways, per, cap, cols, rank, picked, tokens, cotangent,
    mixed, grad_tokens, summed,
    final, x, dy, wu, wd, stage, hid, grad, act, gh, lay, inp, lay_in, inp_in, first, passing,
    local_sems, out_sems, tp_send, tp_recv, ag_send, ag_recv, rs_send, rs_recv, back_send, back_recv,
):
    me_f = lax.axis_index("fsdp")
    me_t = lax.axis_index("tp")
    mine = per * cap
    npc = mine // PIECES
    half = max(1, per // 2)
    rowwise = per % PIECES == 0
    pairs = hid.shape[0]
    rows = n * per
    rpt = rows // ways
    width = rpt * BLK

    def at_position(q):
        q = lax.rem(q + 2 * n, n)
        high = q // (n // 2)
        return 2 * q * (1 - high) + (2 * n - 1 - 2 * q) * high

    odd = lax.rem(me_f, 2)
    here = (me_f // 2) * (1 - odd) + (n - 1 - me_f // 2) * odd
    target = (at_position(here + 1), at_position(here - 1))

    barrier = pltpu.get_barrier_semaphore()
    for f in target:
        pl.semaphore_signal(barrier, inc=1, device_id=(f, me_t), device_id_type=MESH)
    for i in range(1, ways):
        pl.semaphore_signal(
            barrier, inc=1, device_id=(me_f, lax.rem(me_t + i, ways)), device_id_type=MESH
        )

    weights = (wu, wd)
    spot = pl.ds(me_f * mine, mine)
    locals_ = [
        pltpu.make_async_copy(picked.at[pl.ds(0, mine)], wu.at[spot], local_sems.at[0]),
        pltpu.make_async_copy(picked.at[pl.ds(mine, mine)], wd.at[spot], local_sems.at[1]),
        pltpu.make_async_copy(tokens, x.at[me_t], local_sems.at[2]),
        pltpu.make_async_copy(cotangent, dy.at[me_t], local_sems.at[3]),
    ]
    for copy in locals_:
        copy.start()
    locals_[0].wait()
    locals_[2].wait()
    pl.semaphore_wait(barrier, 2 + ways - 1)

    def features(side, i):
        full = (x, dy)[side]
        return pltpu.make_async_remote_copy(
            src_ref=full.at[me_t],
            dst_ref=full.at[me_t],
            send_sem=tp_send.at[side, i],
            recv_sem=tp_recv.at[side, i],
            device_id=(me_f, lax.rem(me_t + i, ways)),
            device_id_type=MESH,
        )

    def hop(side, step, k, d):
        owner = at_position(here - step if d == 0 else here + step)
        block = weights[side].at[pl.ds(owner * mine + k * npc, npc)]
        return pltpu.make_async_remote_copy(
            src_ref=block,
            dst_ref=block,
            send_sem=ag_send.at[side, step, k],
            recv_sem=ag_recv.at[side, step, k],
            device_id=(target[d], me_t),
            device_id_type=MESH,
        )

    def arrived(side, step, k, d):
        owner = at_position(here - step - 1 if d == 0 else here + step + 1)
        block = weights[side].at[pl.ds(owner * mine + k * npc, npc)]
        return pltpu.make_async_remote_copy(
            src_ref=block,
            dst_ref=block,
            send_sem=ag_send.at[side, step, k],
            recv_sem=ag_recv.at[side, step, k],
            device_id=(target[d], me_t),
            device_id_type=MESH,
        )

    order = [(k, k // (PIECES // 2)) for k in range(PIECES)]
    streams = [[(d * (PIECES // 2) + j, d) for d in range(2)] for j in range(PIECES // 2)]

    def gather_start(side, j):
        for k, d in streams[j]:
            hop(side, 0, k, d).start()

    def gather_step(side, step, j):
        for k, d in streams[j]:
            arrived(side, step, k, d).wait_recv()
            hop(side, step + 1, k, d).start()

    def spread(side, row, count):
        total = (hid, grad)[side]
        for i in range(count):
            stage[i, pl.ds(0, cap)] = weights[side][pl.ds((row + i) * cap, cap)]
        full = (x, dy)[side]
        part = full[row // rpt, :, pl.ds(pl.multiple_of(lax.rem(row, rpt) * BLK, BLK), count * BLK)]

        def column(c, carry):
            block = jnp.concatenate(
                [
                    jnp.concatenate(
                        [stage[i, rank[side, row + i, 2 * c + q]] for q in range(2)], axis=1
                    )
                    for i in range(count)
                ],
                axis=0,
            )
            total[c] += jnp.dot(part, block, preferred_element_type=F32)
            return carry

        lax.fori_loop(0, pairs, column, 0)

    def spread_arrived(side, step, d):
        if rowwise:
            owner = at_position(here - step - 1 if d == 0 else here + step + 1)
            spread(side, owner * per + d * half, half)

    def spread_own(side, d):
        if rowwise:
            spread(side, me_f * per + d * half, half)

    def spread_all(side):
        if not rowwise:

            def one(r, carry):
                spread(side, r, 1)
                return carry

            lax.fori_loop(0, rows, one, 0)

    def activate(c):
        v = hid[c]
        s = jnp.tanh(SQRT_TWO_PI * (v + CUBIC * v * v * v))
        a = (0.5 * v * (1.0 + s)).astype(BF16)
        act[2 * c] = a[:, :BLK]
        act[2 * c + 1] = a[:, BLK:]
        hid[c] = 0.5 * (1.0 + s) + 0.5 * v * (1.0 - s * s) * SQRT_TWO_PI * (1.0 + 3.0 * CUBIC * v * v)

    def finish(c, carry):
        g = (grad[c] * hid[c]).astype(BF16)
        gh[2 * c] = g[:, :BLK]
        gh[2 * c + 1] = g[:, BLK:]
        return carry

    def taken(side, start, count):
        values = (gh, act)[side]
        return jnp.concatenate([values[cols[side, start + j]] for j in range(count)], axis=1)

    def back(side, start, stop):
        out = (inp, lay)[side]

        def one(r, carry):
            at = pl.ds(pl.multiple_of(lax.rem(r, rpt) * BLK, BLK), BLK)
            block = jnp.concatenate([weights[side][r * cap + j] for j in range(cap)], axis=1)
            out[r // rpt, :, at] = dot_t(taken(side, r * cap, cap), block).astype(BF16)
            return carry

        lax.fori_loop(jnp.minimum(start, rows), jnp.minimum(stop, rows), one, 0)

    def term(side, owner, k):
        row = owner * per + (k * npc) // cap
        at = pl.ds(pl.multiple_of(lax.rem(row, rpt) * BLK, BLK), BLK)
        left = (x, dy)[side][row // rpt, :, at].T
        return jnp.dot(left, taken(side, owner * mine + k * npc, npc), preferred_element_type=F32)

    def send_sum(side, step, k, d, source):
        return pltpu.make_async_remote_copy(
            src_ref=source,
            dst_ref=passing.at[side, step, k],
            send_sem=rs_send.at[side, step, k],
            recv_sem=rs_recv.at[side, step, k],
            device_id=(target[d], me_t),
            device_id_type=MESH,
        )

    def first_terms(side, j):
        for k, d in streams[j]:
            value = term(side, at_position(here - 1 if d == 0 else here + 1), k).astype(BF16)
            for i in range(npc):
                first[side, k, i] = value[:, i * BLK : (i + 1) * BLK]

    def scatter_start(side, k, d):
        send_sum(side, 0, k, d, first.at[side, k]).start()

    def scatter_step(side, step, j):
        values = [
            term(side, at_position(here - step - 2 if d == 0 else here + step + 2), k)
            for k, d in streams[j]
        ]
        for value, (k, d) in zip(values, streams[j]):
            send_sum(side, step, k, d, passing.at[side, step, k]).wait_recv()
            for i in range(npc):
                passing[side, step, k, i] = (
                    passing[side, step, k, i].astype(F32) + value[:, i * BLK : (i + 1) * BLK]
                ).astype(BF16)
            send_sum(side, step + 1, k, d, passing.at[side, step, k]).start()

    def result(side, k):
        spot = pl.ds(k * npc, npc)
        return pltpu.make_async_copy(final.at[side, spot], summed.at[side, spot], out_sems.at[side, k])

    def scatter_last(side, j, after):
        values = [term(side, me_f, k) for k, d in streams[j]]
        for k, d in streams[j]:
            send_sum(side, n - 2, k, d, passing.at[side, n - 2, k]).wait_recv()
            after(k, d)
        for value, (k, d) in zip(values, streams[j]):
            for i in range(npc):
                final[side, k * npc + i] = (
                    passing[side, n - 2, k, i].astype(F32) + value[:, i * BLK : (i + 1) * BLK]
                )
            result(side, k).start()

    def share(side, i):
        out, into = ((inp, inp_in), (lay, lay_in))[side]
        to = lax.rem(me_t + i, ways)
        return pltpu.make_async_remote_copy(
            src_ref=out.at[to],
            dst_ref=into.at[i - 1],
            send_sem=back_send.at[side, i],
            recv_sem=back_recv.at[side, i],
            device_id=(me_f, to),
            device_id_type=MESH,
        )

    gather_start(0, 0)
    for i in range(1, ways):
        features(0, i).start()
    hid[...] = jnp.zeros_like(hid)
    grad[...] = jnp.zeros_like(grad)
    for i in range(stage.shape[0]):
        stage[i, cap] = jnp.zeros((BLK, BLK), BF16)
    gather_start(0, 1)
    locals_[1].wait()
    locals_[3].wait()
    for step in range(2):
        gather_step(0, step, 0)
        gather_step(0, step, 1)
    for i in range(1, ways):
        features(1, i).start()
    for i in range(1, ways):
        features(0, i).wait_recv()
    for d in range(2):
        spread_own(0, d)

    def up_step(s, carry):
        for j in range(2):
            gather_step(0, s, j)
            spread_arrived(0, s - 2, j)
        return carry

    lax.fori_loop(2, n - 2, up_step, 0)
    for j in range(2):
        for k, d in streams[j]:
            arrived(0, n - 2, k, d).wait_recv()
            hop(1, 0, k, d).start()
        spread_arrived(0, n - 4, j)
        spread_arrived(0, n - 3, j)

    share_act = -(-pairs // (2 * (n - 3)))
    for d in range(2):
        spread_arrived(0, n - 2, d)
    spread_all(0)
    for i in range(1, ways):
        features(1, i).wait_recv()
    for j in range(2):
        gather_step(1, 0, j)
        spread_own(1, j)

    def down_step(s, carry):
        for j in range(2):
            gather_step(1, s, j)
            for i in range(share_act):
                c = ((s - 1) * 2 + j) * share_act + i

                @pl.when(c < pairs)
                def _():
                    activate(c)

            spread_arrived(1, s - 1, j)
        return carry

    lax.fori_loop(1, n - 2, down_step, 0)
    for j in range(2):
        first_terms(1, j)
        for k, d in streams[j]:
            arrived(1, n - 2, k, d).wait_recv()
            scatter_start(1, k, d)
        spread_arrived(1, n - 3, j)
    for d in range(2):
        spread_arrived(1, n - 2, d)
    spread_all(1)

    middle = pairs // 2
    scatter_step(1, 0, 0)
    lax.fori_loop(0, middle, finish, 0)
    scatter_step(1, 0, 1)
    lax.fori_loop(middle, pairs, finish, 0)
    lay_rows = -(-rows // (2 * (n - 3)))

    def down_sum(s, carry):
        for j in range(2):
            scatter_step(1, s, j)
            back(1, ((s - 1) * 2 + j) * lay_rows, ((s - 1) * 2 + j + 1) * lay_rows)
        return carry

    lax.fori_loop(1, n - 2, down_sum, 0)
    for i in range(1, ways):
        share(1, i).start()
    for j in range(2):
        first_terms(0, j)
        scatter_last(1, j, lambda k, d: scatter_start(0, k, d))

    early = max(1, n - 4)
    inp_rows = -(-rows // (2 * early))

    def up_sum(s, carry):
        for j in range(2):
            scatter_step(0, s, j)
            back(0, (s * 2 + j) * inp_rows, (s * 2 + j + 1) * inp_rows)
        return carry

    def up_sum_late(s, carry):
        for j in range(2):
            scatter_step(0, s, j)
        return carry

    def collect(side, out, own, into):
        for i in range(1, ways):
            share(side, i).wait_recv()
        total = own[me_t].astype(F32)
        for i in range(1, ways):
            total += into[i - 1].astype(F32)
        out[...] = total.astype(BF16)

    lax.fori_loop(0, early, up_sum, 0)
    for i in range(1, ways):
        share(0, i).start()
    collect(1, mixed, lay, lay_in)
    lax.fori_loop(early, n - 2, up_sum_late, 0)
    scatter_last(0, 0, lambda k, d: None)
    collect(0, grad_tokens, inp, inp_in)
    scatter_last(0, 1, lambda k, d: None)

    for side in range(2):
        for i in range(1, ways):
            features(side, i).wait_send()
            share(side, i).wait_send()

        def sent(s, carry):
            for k, d in order:
                hop(side, s, k, d).wait_send()
                send_sum(side, s, k, d, passing.at[side, s, k]).wait_send()
            return carry

        lax.fori_loop(0, n - 1, sent, 0)
        for k in range(PIECES):
            result(side, k).wait()


def fused(cols, rank, picked, tokens, cotangent, n, ways, per, cap, col_blocks):
    group, width = tokens.shape
    rows = n * per
    npc = per * cap // PIECES
    half = max(1, per // 2)
    vmem = pl.BlockSpec(memory_space=pltpu.VMEM)
    smem = pl.BlockSpec(memory_space=pltpu.SMEM)
    hbm = pl.BlockSpec(memory_space=pl.ANY)
    dma = pltpu.SemaphoreType.DMA
    return pl.pallas_call(
        functools.partial(fused_kernel, n, ways, per, cap),
        out_shape=(
            jax.ShapeDtypeStruct((group, width), BF16),
            jax.ShapeDtypeStruct((group, width), BF16),
            jax.ShapeDtypeStruct((2, per * cap, BLK, BLK), F32),
        ),
        in_specs=[smem, smem, hbm, hbm, hbm],
        out_specs=(vmem, vmem, hbm),
        scratch_shapes=[
            pltpu.VMEM((2, per * cap, BLK, BLK), F32),
            pltpu.VMEM((ways, group, width), BF16),
            pltpu.VMEM((ways, group, width), BF16),
            pltpu.VMEM((rows * cap, BLK, BLK), BF16),
            pltpu.VMEM((rows * cap, BLK, BLK), BF16),
            pltpu.VMEM((half, cap + 1, BLK, BLK), BF16),
            pltpu.VMEM((col_blocks // 2, group, 2 * BLK), F32),
            pltpu.VMEM((col_blocks // 2, group, 2 * BLK), F32),
            pltpu.VMEM((col_blocks, group, BLK), BF16),
            pltpu.VMEM((col_blocks, group, BLK), BF16),
            pltpu.VMEM((ways, group, width), BF16),
            pltpu.VMEM((ways, group, width), BF16),
            pltpu.VMEM((ways - 1, group, width), BF16),
            pltpu.VMEM((ways - 1, group, width), BF16),
            pltpu.VMEM((2, PIECES, npc, BLK, BLK), BF16),
            pltpu.VMEM((2, n - 1, PIECES, npc, BLK, BLK), BF16),
            dma((4,)),
            dma((2, PIECES)),
            dma((2, ways)),
            dma((2, ways)),
            dma((2, n - 1, PIECES)),
            dma((2, n - 1, PIECES)),
            dma((2, n - 1, PIECES)),
            dma((2, n - 1, PIECES)),
            dma((2, ways)),
            dma((2, ways)),
        ],
        compiler_params=pltpu.CompilerParams(
            collective_id=0, has_side_effects=True, vmem_limit_bytes=63 << 20
        ),
        name="fused_layer",
    )(cols, rank, picked, tokens, cotangent)


def body(tokens, cotangent, up_weight, down_weight, up_list, up_count, down_list, down_count):
    per = up_weight.shape[0] // BLK
    col_blocks = up_weight.shape[1] // BLK
    owners = lax.axis_size("fsdp")
    rows = per * owners
    cap = up_list.shape[1] // rows
    mine = per * cap
    entries = jnp.stack([up_list[0], down_list[0]])
    counts = jnp.stack([up_count[0], down_count[0]])
    cols, rank = tables(entries, counts, rows, col_blocks, cap)
    my_cols = lax.dynamic_slice_in_dim(cols, lax.axis_index("fsdp") * mine, mine, axis=1)
    picked = pick(my_cols, up_weight, down_weight, cap)
    mixed, grad_tokens, summed = fused(
        jnp.maximum(cols, 0), rank, picked, tokens, cotangent,
        owners, lax.axis_size("tp"), per, cap, col_blocks,
    )
    grad_up, grad_down, mixed, grad_tokens = place(
        my_cols, summed, mixed, grad_tokens, cap, col_blocks
    )
    return (mixed, grad_tokens, grad_up, grad_down)


def solution(mesh):
    return jax.shard_map(
        body,
        mesh=mesh,
        in_specs=(
            P("fsdp", "tp"),
            P("fsdp", "tp"),
            P("fsdp", "tp"),
            P("fsdp", "tp"),
            P("tp", None, None),
            P("tp"),
            P("tp", None, None),
            P("tp"),
        ),
        out_specs=(P("fsdp", "tp"), P("fsdp", "tp"), P("fsdp", "tp"), P("fsdp", "tp")),
        check_vma=False,
    )
```

```python
import functools

import jax
import jax.numpy as jnp
from jax import lax
from jax.experimental import pallas as pl
from jax.experimental.pallas import tpu as pltpu
from jax.sharding import PartitionSpec as P

BLK = 128
SQRT_TWO_PI = 0.7978845608028654
CUBIC = 0.044715
F32 = jnp.float32
BF16 = jnp.bfloat16


def tables(entries, counts, row_blocks, col_blocks, cap):
    length = entries.shape[1]
    rows, cols = entries[:, :, 0], entries[:, :, 1]
    at = jnp.arange(length, dtype=jnp.int32)
    valid = at[None, :] < counts[:, None]
    earlier = (rows[:, :, None] == rows[:, None, :]) & (at[None, None, :] < at[None, :, None])
    rank = jnp.sum((earlier & valid[:, None, :]).astype(jnp.int32), axis=2)
    slot = jnp.where(valid, rows * cap + rank, -1)
    slots = jnp.arange(row_blocks * cap, dtype=jnp.int32)
    chosen = slot[:, None, :] == slots[None, :, None]
    slot_cols = jnp.sum(jnp.where(chosen, cols[:, None, :] + 1, 0), axis=2) - 1
    place = jnp.where(valid, rows * col_blocks + cols, -1)
    places = jnp.arange(row_blocks * col_blocks, dtype=jnp.int32)
    here = place[:, None, :] == places[None, :, None]
    rank_of = jnp.sum(jnp.where(here, rank[:, None, :] - cap, 0), axis=2) + cap
    return slot_cols, rank_of.reshape(entries.shape[0], row_blocks, col_blocks)


def pick_kernel(
    cap, cols_ref, up_ref, down_ref, out_ref, zero_up, zero_down, zeros, sems, zero_sems
):
    count = out_ref.shape[0] // 2
    blanks = [
        pltpu.make_async_copy(zeros, out.at[pl.ds(i * BLK, BLK)], zero_sems.at[side, i])
        for side, out in enumerate((zero_up, zero_down))
        for i in range(count // cap)
    ]
    for side, weight in enumerate((up_ref, down_ref)):
        for s in range(count):
            col = pl.multiple_of(jnp.maximum(cols_ref[side, s], 0) * BLK, BLK)
            pltpu.make_async_copy(
                weight.at[pl.ds((s // cap) * BLK, BLK), pl.ds(col, BLK)],
                out_ref.at[side * count + s],
                sems.at[side * count + s],
            ).start()
    zeros[...] = jnp.zeros_like(zeros)
    for blank in blanks:
        blank.start()
    for side, weight in enumerate((up_ref, down_ref)):
        for s in range(count):
            pltpu.make_async_copy(
                weight.at[pl.ds((s // cap) * BLK, BLK), pl.ds(0, BLK)],
                out_ref.at[side * count + s],
                sems.at[side * count + s],
            ).wait()

            @pl.when(cols_ref[side, s] < 0)
            def _():
                out_ref[side * count + s] = jnp.zeros((BLK, BLK), BF16)

    for blank in blanks:
        blank.wait()


def pick(cols, up_weight, down_weight, cap):
    count = cols.shape[1]
    blank = jax.ShapeDtypeStruct(up_weight.shape, F32)
    hbm = pl.BlockSpec(memory_space=pl.ANY)
    return pl.pallas_call(
        functools.partial(pick_kernel, cap),
        out_shape=(jax.ShapeDtypeStruct((2 * count, BLK, BLK), BF16), blank, blank),
        in_specs=[pl.BlockSpec(memory_space=pltpu.SMEM), hbm, hbm],
        out_specs=(pl.BlockSpec(memory_space=pltpu.VMEM), hbm, hbm),
        scratch_shapes=[
            pltpu.VMEM((BLK, up_weight.shape[1]), F32),
            pltpu.SemaphoreType.DMA((2 * count,)),
            pltpu.SemaphoreType.DMA((2, count // cap)),
        ],
        compiler_params=pltpu.CompilerParams(vmem_limit_bytes=60 << 20),
        name="pick_blocks",
    )(cols, up_weight, down_weight)


def place_kernel(
    cap, cols_ref, sum_ref, mixed_in, grad_in, zero_up, zero_down,
    up_ref, down_ref, mixed_out, grad_out, sems, pass_sems,
):
    del zero_up, zero_down
    through = [
        pltpu.make_async_copy(mixed_in, mixed_out, pass_sems.at[0]),
        pltpu.make_async_copy(grad_in, grad_out, pass_sems.at[1]),
    ]
    for copy in through:
        copy.start()
    count = cols_ref.shape[1]

    def move(side, out, s):
        col = pl.multiple_of(jnp.maximum(cols_ref[side, s], 0) * BLK, BLK)
        return pltpu.make_async_copy(
            sum_ref.at[side, s],
            out.at[pl.ds((s // cap) * BLK, BLK), pl.ds(col, BLK)],
            sems.at[side, s],
        )

    for side, out in enumerate((up_ref, down_ref)):
        for s in range(count):

            @pl.when(cols_ref[side, s] >= 0)
            def _():
                move(side, out, s).start()

    for side, out in enumerate((up_ref, down_ref)):
        for s in range(count):

            @pl.when(cols_ref[side, s] >= 0)
            def _():
                move(side, out, s).wait()

    for copy in through:
        copy.wait()


def place(cols, summed, mixed, grad_tokens, zero_up, zero_down, cap):
    hbm = pl.BlockSpec(memory_space=pl.ANY)
    grad = jax.ShapeDtypeStruct(zero_up.shape, F32)
    same = jax.ShapeDtypeStruct(mixed.shape, BF16)
    return pl.pallas_call(
        functools.partial(place_kernel, cap),
        out_shape=(grad, grad, same, same),
        in_specs=[pl.BlockSpec(memory_space=pltpu.SMEM)] + [hbm] * 5,
        out_specs=(hbm,) * 4,
        input_output_aliases={4: 0, 5: 1},
        scratch_shapes=[
            pltpu.SemaphoreType.DMA(cols.shape),
            pltpu.SemaphoreType.DMA((2,)),
        ],
        compiler_params=pltpu.CompilerParams(vmem_limit_bytes=60 << 20),
        name="place_grads",
    )(cols, summed, mixed, grad_tokens, zero_up, zero_down)


MESH = pl.DeviceIdType.MESH
PIECES = 4


def dot_t(left, right):
    return lax.dot_general(left, right, (((1,), (1,)), ((), ())), preferred_element_type=F32)


def fused_kernel(
    n, ways, per, cap, cols, rank, picked, tokens, cotangent,
    mixed, grad_tokens, summed,
    final, x, dy, wu, wd, stage, hid, grad, act, gh, lay, inp, lay_in, inp_in, first, passing,
    local_sems, out_sems, tp_send, tp_recv, ag_send, ag_recv, rs_send, rs_recv, back_send, back_recv,
):
    me_f = lax.axis_index("fsdp")
    me_t = lax.axis_index("tp")
    mine = per * cap
    npc = mine // PIECES
    half = max(1, per // 2)
    rowwise = per % PIECES == 0
    pairs = hid.shape[0]
    rows = n * per
    rpt = rows // ways
    width = rpt * BLK

    def at_position(q):
        q = lax.rem(q + 2 * n, n)
        high = q // (n // 2)
        return 2 * q * (1 - high) + (2 * n - 1 - 2 * q) * high

    odd = lax.rem(me_f, 2)
    here = (me_f // 2) * (1 - odd) + (n - 1 - me_f // 2) * odd
    target = (at_position(here + 1), at_position(here - 1))

    barrier = pltpu.get_barrier_semaphore()
    for f in target:
        pl.semaphore_signal(barrier, inc=1, device_id=(f, me_t), device_id_type=MESH)
    for i in range(1, ways):
        pl.semaphore_signal(
            barrier, inc=1, device_id=(me_f, lax.rem(me_t + i, ways)), device_id_type=MESH
        )

    weights = (wu, wd)
    spot = pl.ds(me_f * mine, mine)
    locals_ = [
        pltpu.make_async_copy(picked.at[pl.ds(0, mine)], wu.at[spot], local_sems.at[0]),
        pltpu.make_async_copy(picked.at[pl.ds(mine, mine)], wd.at[spot], local_sems.at[1]),
        pltpu.make_async_copy(tokens, x.at[me_t], local_sems.at[2]),
        pltpu.make_async_copy(cotangent, dy.at[me_t], local_sems.at[3]),
    ]
    for copy in locals_:
        copy.start()
    locals_[0].wait()
    locals_[2].wait()
    pl.semaphore_wait(barrier, 2 + ways - 1)

    def features(side, i):
        full = (x, dy)[side]
        return pltpu.make_async_remote_copy(
            src_ref=full.at[me_t],
            dst_ref=full.at[me_t],
            send_sem=tp_send.at[side, i],
            recv_sem=tp_recv.at[side, i],
            device_id=(me_f, lax.rem(me_t + i, ways)),
            device_id_type=MESH,
        )

    def hop(side, step, k, d):
        owner = at_position(here - step if d == 0 else here + step)
        block = weights[side].at[pl.ds(owner * mine + k * npc, npc)]
        return pltpu.make_async_remote_copy(
            src_ref=block,
            dst_ref=block,
            send_sem=ag_send.at[side, step, k],
            recv_sem=ag_recv.at[side, step, k],
            device_id=(target[d], me_t),
            device_id_type=MESH,
        )

    def arrived(side, step, k, d):
        owner = at_position(here - step - 1 if d == 0 else here + step + 1)
        block = weights[side].at[pl.ds(owner * mine + k * npc, npc)]
        return pltpu.make_async_remote_copy(
            src_ref=block,
            dst_ref=block,
            send_sem=ag_send.at[side, step, k],
            recv_sem=ag_recv.at[side, step, k],
            device_id=(target[d], me_t),
            device_id_type=MESH,
        )

    order = [(k, k // (PIECES // 2)) for k in range(PIECES)]
    streams = [[(d * (PIECES // 2) + j, d) for d in range(2)] for j in range(PIECES // 2)]

    def gather_start(side, j):
        for k, d in streams[j]:
            hop(side, 0, k, d).start()

    def gather_step(side, step, j):
        for k, d in streams[j]:
            arrived(side, step, k, d).wait_recv()
            hop(side, step + 1, k, d).start()

    def spread(side, row, count):
        total = (hid, grad)[side]
        for i in range(count):
            stage[i, pl.ds(0, cap)] = weights[side][pl.ds((row + i) * cap, cap)]
        full = (x, dy)[side]
        part = full[row // rpt, :, pl.ds(pl.multiple_of(lax.rem(row, rpt) * BLK, BLK), count * BLK)]

        def column(c, carry):
            block = jnp.concatenate(
                [
                    jnp.concatenate(
                        [stage[i, rank[side, row + i, 2 * c + q]] for q in range(2)], axis=1
                    )
                    for i in range(count)
                ],
                axis=0,
            )
            total[c] += jnp.dot(part, block, preferred_element_type=F32)
            return carry

        lax.fori_loop(0, pairs, column, 0)

    def spread_arrived(side, step, d):
        if rowwise:
            owner = at_position(here - step - 1 if d == 0 else here + step + 1)
            spread(side, owner * per + d * half, half)

    def spread_own(side, d):
        if rowwise:
            spread(side, me_f * per + d * half, half)

    def spread_all(side):
        if not rowwise:

            def one(r, carry):
                spread(side, r, 1)
                return carry

            lax.fori_loop(0, rows, one, 0)

    def activate(c):
        v = hid[c]
        s = jnp.tanh(SQRT_TWO_PI * (v + CUBIC * v * v * v))
        a = (0.5 * v * (1.0 + s)).astype(BF16)
        act[2 * c] = a[:, :BLK]
        act[2 * c + 1] = a[:, BLK:]
        hid[c] = 0.5 * (1.0 + s) + 0.5 * v * (1.0 - s * s) * SQRT_TWO_PI * (1.0 + 3.0 * CUBIC * v * v)

    def finish(c, carry):
        g = (grad[c] * hid[c]).astype(BF16)
        gh[2 * c] = g[:, :BLK]
        gh[2 * c + 1] = g[:, BLK:]
        return carry

    def taken(side, start, count):
        values = (gh, act)[side]
        return jnp.concatenate([values[cols[side, start + j]] for j in range(count)], axis=1)

    def back(side, start, stop):
        out = (inp, lay)[side]

        def one(r, carry):
            at = pl.ds(pl.multiple_of(lax.rem(r, rpt) * BLK, BLK), BLK)
            block = jnp.concatenate([weights[side][r * cap + j] for j in range(cap)], axis=1)
            out[r // rpt, :, at] = dot_t(taken(side, r * cap, cap), block).astype(BF16)
            return carry

        lax.fori_loop(jnp.minimum(start, rows), jnp.minimum(stop, rows), one, 0)

    def term(side, owner, k):
        row = owner * per + (k * npc) // cap
        at = pl.ds(pl.multiple_of(lax.rem(row, rpt) * BLK, BLK), BLK)
        left = (x, dy)[side][row // rpt, :, at].T
        return jnp.dot(left, taken(side, owner * mine + k * npc, npc), preferred_element_type=F32)

    def send_sum(side, step, k, d, source):
        return pltpu.make_async_remote_copy(
            src_ref=source,
            dst_ref=passing.at[side, step, k],
            send_sem=rs_send.at[side, step, k],
            recv_sem=rs_recv.at[side, step, k],
            device_id=(target[d], me_t),
            device_id_type=MESH,
        )

    def first_terms(side, j):
        for k, d in streams[j]:
            value = term(side, at_position(here - 1 if d == 0 else here + 1), k).astype(BF16)
            for i in range(npc):
                first[side, k, i] = value[:, i * BLK : (i + 1) * BLK]

    def scatter_start(side, k, d):
        send_sum(side, 0, k, d, first.at[side, k]).start()

    def scatter_step(side, step, j):
        values = [
            term(side, at_position(here - step - 2 if d == 0 else here + step + 2), k)
            for k, d in streams[j]
        ]
        for value, (k, d) in zip(values, streams[j]):
            send_sum(side, step, k, d, passing.at[side, step, k]).wait_recv()
            for i in range(npc):
                passing[side, step, k, i] = (
                    passing[side, step, k, i].astype(F32) + value[:, i * BLK : (i + 1) * BLK]
                ).astype(BF16)
            send_sum(side, step + 1, k, d, passing.at[side, step, k]).start()

    def result(side, k):
        spot = pl.ds(k * npc, npc)
        return pltpu.make_async_copy(final.at[side, spot], summed.at[side, spot], out_sems.at[side, k])

    def scatter_last(side, j, after):
        values = [term(side, me_f, k) for k, d in streams[j]]
        for k, d in streams[j]:
            send_sum(side, n - 2, k, d, passing.at[side, n - 2, k]).wait_recv()
            after(k, d)
        for value, (k, d) in zip(values, streams[j]):
            for i in range(npc):
                final[side, k * npc + i] = (
                    passing[side, n - 2, k, i].astype(F32) + value[:, i * BLK : (i + 1) * BLK]
                )
            result(side, k).start()

    def share(side, i):
        out, into = ((inp, inp_in), (lay, lay_in))[side]
        to = lax.rem(me_t + i, ways)
        return pltpu.make_async_remote_copy(
            src_ref=out.at[to],
            dst_ref=into.at[i - 1],
            send_sem=back_send.at[side, i],
            recv_sem=back_recv.at[side, i],
            device_id=(me_f, to),
            device_id_type=MESH,
        )

    gather_start(0, 0)
    for i in range(1, ways):
        features(0, i).start()
    hid[...] = jnp.zeros_like(hid)
    grad[...] = jnp.zeros_like(grad)
    for i in range(stage.shape[0]):
        stage[i, cap] = jnp.zeros((BLK, BLK), BF16)
    gather_start(0, 1)
    locals_[1].wait()
    locals_[3].wait()
    for step in range(2):
        gather_step(0, step, 0)
        gather_step(0, step, 1)
    for i in range(1, ways):
        features(1, i).start()
    for i in range(1, ways):
        features(0, i).wait_recv()
    for d in range(2):
        spread_own(0, d)

    def up_step(s, carry):
        for j in range(2):
            gather_step(0, s, j)
            spread_arrived(0, s - 2, j)
        return carry

    lax.fori_loop(2, n - 2, up_step, 0)
    for j in range(2):
        for k, d in streams[j]:
            arrived(0, n - 2, k, d).wait_recv()
            hop(1, 0, k, d).start()
        spread_arrived(0, n - 4, j)
        spread_arrived(0, n - 3, j)

    share_act = -(-pairs // (2 * (n - 3)))
    for d in range(2):
        spread_arrived(0, n - 2, d)
    spread_all(0)
    for i in range(1, ways):
        features(1, i).wait_recv()
    for j in range(2):
        gather_step(1, 0, j)
        spread_own(1, j)

    def down_step(s, carry):
        for j in range(2):
            gather_step(1, s, j)
            for i in range(share_act):
                c = ((s - 1) * 2 + j) * share_act + i

                @pl.when(c < pairs)
                def _():
                    activate(c)

            spread_arrived(1, s - 1, j)
        return carry

    lax.fori_loop(1, n - 2, down_step, 0)
    for j in range(2):
        first_terms(1, j)
        for k, d in streams[j]:
            arrived(1, n - 2, k, d).wait_recv()
            scatter_start(1, k, d)
        spread_arrived(1, n - 3, j)
    for d in range(2):
        spread_arrived(1, n - 2, d)
    spread_all(1)

    middle = pairs // 2
    scatter_step(1, 0, 0)
    lax.fori_loop(0, middle, finish, 0)
    scatter_step(1, 0, 1)
    lax.fori_loop(middle, pairs, finish, 0)
    lay_rows = -(-rows // (2 * (n - 3)))

    def down_sum(s, carry):
        for j in range(2):
            scatter_step(1, s, j)
            back(1, ((s - 1) * 2 + j) * lay_rows, ((s - 1) * 2 + j + 1) * lay_rows)
        return carry

    lax.fori_loop(1, n - 2, down_sum, 0)
    for i in range(1, ways):
        share(1, i).start()
    for j in range(2):
        first_terms(0, j)
        scatter_last(1, j, lambda k, d: scatter_start(0, k, d))

    early = max(1, n - 4)
    inp_rows = -(-rows // (2 * early))

    def up_sum(s, carry):
        for j in range(2):
            scatter_step(0, s, j)
            back(0, (s * 2 + j) * inp_rows, (s * 2 + j + 1) * inp_rows)
        return carry

    def up_sum_late(s, carry):
        for j in range(2):
            scatter_step(0, s, j)
        return carry

    def collect(side, out, own, into):
        for i in range(1, ways):
            share(side, i).wait_recv()
        total = own[me_t].astype(F32)
        for i in range(1, ways):
            total += into[i - 1].astype(F32)
        out[...] = total.astype(BF16)

    lax.fori_loop(0, early, up_sum, 0)
    for i in range(1, ways):
        share(0, i).start()
    collect(1, mixed, lay, lay_in)
    lax.fori_loop(early, n - 2, up_sum_late, 0)
    scatter_last(0, 0, lambda k, d: None)
    collect(0, grad_tokens, inp, inp_in)
    scatter_last(0, 1, lambda k, d: None)

    for side in range(2):
        for i in range(1, ways):
            features(side, i).wait_send()
            share(side, i).wait_send()

        def sent(s, carry):
            for k, d in order:
                hop(side, s, k, d).wait_send()
                send_sum(side, s, k, d, passing.at[side, s, k]).wait_send()
            return carry

        lax.fori_loop(0, n - 1, sent, 0)
        for k in range(PIECES):
            result(side, k).wait()


def fused(cols, rank, picked, tokens, cotangent, n, ways, per, cap, col_blocks):
    group, width = tokens.shape
    rows = n * per
    npc = per * cap // PIECES
    half = max(1, per // 2)
    vmem = pl.BlockSpec(memory_space=pltpu.VMEM)
    smem = pl.BlockSpec(memory_space=pltpu.SMEM)
    hbm = pl.BlockSpec(memory_space=pl.ANY)
    dma = pltpu.SemaphoreType.DMA
    return pl.pallas_call(
        functools.partial(fused_kernel, n, ways, per, cap),
        out_shape=(
            jax.ShapeDtypeStruct((group, width), BF16),
            jax.ShapeDtypeStruct((group, width), BF16),
            jax.ShapeDtypeStruct((2, per * cap, BLK, BLK), F32),
        ),
        in_specs=[smem, smem, hbm, hbm, hbm],
        out_specs=(vmem, vmem, hbm),
        scratch_shapes=[
            pltpu.VMEM((2, per * cap, BLK, BLK), F32),
            pltpu.VMEM((ways, group, width), BF16),
            pltpu.VMEM((ways, group, width), BF16),
            pltpu.VMEM((rows * cap, BLK, BLK), BF16),
            pltpu.VMEM((rows * cap, BLK, BLK), BF16),
            pltpu.VMEM((half, cap + 1, BLK, BLK), BF16),
            pltpu.VMEM((col_blocks // 2, group, 2 * BLK), F32),
            pltpu.VMEM((col_blocks // 2, group, 2 * BLK), F32),
            pltpu.VMEM((col_blocks, group, BLK), BF16),
            pltpu.VMEM((col_blocks, group, BLK), BF16),
            pltpu.VMEM((ways, group, width), BF16),
            pltpu.VMEM((ways, group, width), BF16),
            pltpu.VMEM((ways - 1, group, width), BF16),
            pltpu.VMEM((ways - 1, group, width), BF16),
            pltpu.VMEM((2, PIECES, npc, BLK, BLK), BF16),
            pltpu.VMEM((2, n - 1, PIECES, npc, BLK, BLK), BF16),
            dma((4,)),
            dma((2, PIECES)),
            dma((2, ways)),
            dma((2, ways)),
            dma((2, n - 1, PIECES)),
            dma((2, n - 1, PIECES)),
            dma((2, n - 1, PIECES)),
            dma((2, n - 1, PIECES)),
            dma((2, ways)),
            dma((2, ways)),
        ],
        compiler_params=pltpu.CompilerParams(
            collective_id=0, has_side_effects=True, vmem_limit_bytes=63 << 20
        ),
        name="fused_layer",
    )(cols, rank, picked, tokens, cotangent)


def body(tokens, cotangent, up_weight, down_weight, up_list, up_count, down_list, down_count):
    per = up_weight.shape[0] // BLK
    col_blocks = up_weight.shape[1] // BLK
    owners = lax.axis_size("fsdp")
    rows = per * owners
    cap = up_list.shape[1] // rows
    mine = per * cap
    entries = jnp.stack([up_list[0], down_list[0]])
    counts = jnp.stack([up_count[0], down_count[0]])
    cols, rank = tables(entries, counts, rows, col_blocks, cap)
    my_cols = lax.dynamic_slice_in_dim(cols, lax.axis_index("fsdp") * mine, mine, axis=1)
    picked, zero_up, zero_down = pick(my_cols, up_weight, down_weight, cap)
    mixed, grad_tokens, summed = fused(
        jnp.maximum(cols, 0), rank, picked, tokens, cotangent,
        owners, lax.axis_size("tp"), per, cap, col_blocks,
    )
    grad_up, grad_down, mixed, grad_tokens = place(
        my_cols, summed, mixed, grad_tokens, zero_up, zero_down, cap
    )
    return (mixed, grad_tokens, grad_up, grad_down)


def solution(mesh):
    return jax.shard_map(
        body,
        mesh=mesh,
        in_specs=(
            P("fsdp", "tp"),
            P("fsdp", "tp"),
            P("fsdp", "tp"),
            P("fsdp", "tp"),
            P("tp", None, None),
            P("tp"),
            P("tp", None, None),
            P("tp"),
        ),
        out_specs=(P("fsdp", "tp"), P("fsdp", "tp"), P("fsdp", "tp"), P("fsdp", "tp")),
        check_vma=False,
    )
```
